128 devices in a mesh: row: 16 (over z, x), col: 8 (over y, core).
Axes of the slice: x: 4, y: 4, z: 4, core: 2. Of those that a mesh axis runs over, the one named last changes fastest.
Arguments:
- targets: float32 [10, 1024, 1024], P(None, 'row', 'col'), may hold values from -6 to 6
- lower_panel: float32 [10, 1024, 29696], P(None, 'row', 'col'), may hold values from -0.03125 to 0.03125
- prior_solution: float32 [29696, 1024], P('col', 'row'), may hold values from -6 to 6
- diag_inverse: float32 [10, 1024, 1024], P(None, 'row'), may hold values from -2 to 2, as said below
- below_blocks: float32 [45, 1024, 1024], P(None, 'row'), may hold values from -0.1875 to 0.1875
Outputs:
- solution: float32 [10, 1024, 1024], P(None, 'row', 'col')
The draws below stay inside these ranges and needn't reach their ends.
Inputs may be any that keep to these rules, and one draw needn't show every extreme that they name: `diag_inverse`: each block is lower triangular with a positive diagonal.
All inputs are finite; a program needn't handle non-finite values.
Results may differ from the reference program's by a relative error of at most 0.00019.
Values sent between devices are 32-bit elements; how exact they have to be, the bound alone decides.
A program may use at most 192 MiB of HBM per device.

```python
import math
import jax
import jax.numpy as jnp
from jax import lax

NB = 1024
STEPS = 10
R = 1024
PRIOR = 29696
PAIRS = 45


def draw_diag_inverse(key, part):
    key = jax.random.fold_in(key, 7)
    first_key, second_key = jax.random.split(key)
    shape = (STEPS, NB, NB)
    row_ids = lax.broadcasted_iota(jnp.int32, shape, 1)
    col_ids = lax.broadcasted_iota(jnp.int32, shape, 2)
    noise = jax.random.normal(first_key, shape, jnp.float32)
    diagonal = jax.random.uniform(second_key, (STEPS, NB, 1), jnp.float32, 0.7, 1.4)
    below = jnp.where(col_ids < row_ids, noise * (0.6 / math.sqrt(NB)), 0.0)
    return below + jnp.where(col_ids == row_ids, diagonal, 0.0)


def block_scale(stream_key, extent, shards, least, largest):
    def one(position, parts):
        draws = jax.random.uniform(jax.random.fold_in(jax.random.fold_in(stream_key, 6), position), (parts,), jnp.float32, least / len(shards), largest / len(shards))
        return jnp.repeat(jnp.exp(draws), extent[position] // parts).reshape((-1,) + (1,) * (len(extent) - position - 1))

    gain = one(*shards[0])
    for cut in shards[1:]:
        gain = gain * one(*cut)
    return gain


def normal_values(own_key, dims, scale, limit, shards=(), held_as=jnp.bfloat16):
    drawn = scale * jax.random.normal(own_key, dims, jnp.float32)
    if shards:
        drawn = drawn * block_scale(own_key, dims, shards, -0.22, 0.18)
    return jnp.clip(drawn, -limit, limit).astype(held_as)


def setup_inputs(seed: int = 0) -> dict:
    seeds = jax.random.split(jax.random.key(seed), 6)
    return {
        "targets": normal_values(seeds[0], (STEPS, NB, R), 1.0, 6.0, ((1, 16), (2, 8)), jnp.float32),
        "lower_panel": normal_values(seeds[1], (STEPS, NB, PRIOR), PRIOR ** -0.5, 0.03125, ((1, 16), (2, 8)), jnp.float32),
        "prior_solution": normal_values(seeds[2], (PRIOR, R), 1.0, 6.0, ((0, 8), (1, 16)), jnp.float32),
        "diag_inverse": draw_diag_inverse(jax.random.fold_in(seeds[5], 71), 0),
        "below_blocks": normal_values(seeds[4], (PAIRS, NB, NB), NB ** -0.5, 0.1875, ((1, 16),), jnp.float32),
    }


def product(left, right):
    return jnp.dot(left, right, precision=lax.Precision.HIGHEST, preferred_element_type=jnp.float32)


def reference(targets, lower_panel, prior_solution, diag_inverse, below_blocks):
    solved = []
    for k in range(STEPS):
        remainder = targets[k] - product(lower_panel[k], prior_solution)
        for j in range(k):
            remainder = remainder - product(below_blocks[k * (k - 1) // 2 + j], solved[j])
        solved.append(product(diag_inverse[k], remainder))
    return jnp.stack(solved)
```

```python
import jax
import jax.numpy as jnp
from jax import lax
from jax.experimental import pallas as pl
from jax.experimental.pallas import tpu as pltpu
from jax.sharding import PartitionSpec as P

MESH = pl.DeviceIdType.MESH
STEPS = 10
ROWS = 16


def product(left, right):
    return jnp.dot(left, right, precision=lax.Precision.HIGHEST, preferred_element_type=jnp.float32)


def split(value):
    high = value.astype(jnp.bfloat16)
    return high, (value - high.astype(jnp.float32)).astype(jnp.bfloat16)


def dot(left, right):
    return jnp.dot(left, right, preferred_element_type=jnp.float32)


def solve_kernel(rhs_ref, diag_ref, coupling_ref, out_ref, held, own, weights, send_sem, recv_sem):
    row = lax.axis_index("row")
    barrier = pltpu.get_barrier_semaphore()
    for d in range(1, ROWS):
        pl.semaphore_signal(barrier, inc=1, device_id={"row": lax.rem(row + d, ROWS)}, device_id_type=MESH)
    pl.semaphore_wait(barrier, ROWS - 1)

    def copy(k, d):
        return pltpu.make_async_remote_copy(
            src_ref=own.at[k],
            dst_ref=held.at[k, row],
            send_sem=send_sem.at[lax.rem(k, 2), d],
            recv_sem=recv_sem.at[lax.rem(k, 2), d],
            device_id={"row": lax.rem(row + d, ROWS)},
            device_id_type=MESH,
        )

    def send(k):
        for d in range(1, ROWS):
            copy(k, d).start()
        held[k, row] = own[k]

    def arrive(k):
        for d in range(1, ROWS):
            copy(k, d).wait_recv()
        high, low = split(held[k].reshape(ROWS * held.shape[2], held.shape[3]))
        weights[...] = jnp.concatenate([high, low], axis=1)

    def times(block):
        high, low = split(block)
        both = dot(high, weights[...])
        return both[:, :128] + both[:, 128:] + dot(low, weights[:, :128])

    def coupling(i, k):
        pair = i * (i - 1) // 2 + k
        return jnp.concatenate([coupling_ref[c, pair] for c in range(8)], axis=1)

    own[...] = rhs_ref[...]
    send(0)

    def step(k, carry):
        arrive(k)
        own[k + 1] -= times(coupling(k + 1, k))
        send(k + 1)
        out_ref[k] = times(diag_ref[k])

        def later(i, carry):
            own[i] -= times(coupling(i, k))
            return carry

        lax.fori_loop(k + 2, STEPS, later, 0)
        for d in range(1, ROWS):
            copy(k, d).wait_send()
        return carry

    lax.fori_loop(0, STEPS - 1, step, 0)
    arrive(STEPS - 1)
    out_ref[STEPS - 1] = times(diag_ref[STEPS - 1])
    for d in range(1, ROWS):
        copy(STEPS - 1, d).wait_send()


def solve(rhs, diag, coupling):
    steps, rows, columns = rhs.shape
    return pl.pallas_call(
        solve_kernel,
        out_shape=jax.ShapeDtypeStruct(rhs.shape, jnp.float32),
        in_specs=[pl.BlockSpec(memory_space=pltpu.VMEM)] * 3,
        out_specs=pl.BlockSpec(memory_space=pltpu.VMEM),
        scratch_shapes=[
            pltpu.VMEM((steps, ROWS, rows, columns), jnp.float32),
            pltpu.VMEM((steps, rows, columns), jnp.float32),
            pltpu.VMEM((ROWS * rows, 2 * columns), jnp.bfloat16),
            pltpu.SemaphoreType.DMA((2, ROWS)),
            pltpu.SemaphoreType.DMA((2, ROWS)),
        ],
        compiler_params=pltpu.CompilerParams(
            collective_id=1, has_side_effects=True, vmem_limit_bytes=48 << 20
        ),
    )(rhs, diag, coupling)


def on_device(targets, lower_panel, prior_solution, diag_inverse, below_blocks):
    step_count, row_count, prior_width = lower_panel.shape
    col = lax.axis_index("col")
    width = diag_inverse.shape[2] // 8
    diag_part = lax.dynamic_slice_in_dim(diag_inverse, col * width, width, 2)
    diag_columns = lax.all_gather(diag_part, "row", axis=1, tiled=True)
    parts = []
    for i in range(1, step_count):
        for j in range(i):
            parts.append(product(below_blocks[i * (i - 1) // 2 + j], diag_columns[j]))
    coupling = lax.all_gather(jnp.stack(parts), "col", axis=0)
    flattened = lower_panel.reshape(step_count * row_count, prior_width)
    partial_value = product(flattened, lax.all_gather(prior_solution, "row", axis=1, tiled=True))
    reduced = lax.psum_scatter(partial_value, "col", scatter_dimension=1, tiled=True).reshape(
        step_count, row_count, -1
    )
    return solve(targets - reduced, diag_inverse, coupling)


def solution(mesh):
    in_specs = (
        P(None, "row", "col"),
        P(None, "row", "col"),
        P("col", "row"),
        P(None, "row", None),
        P(None, "row", None),
    )
    out_specs = P(None, "row", "col")
    return jax.shard_map(
        on_device, mesh=mesh, in_specs=in_specs, out_specs=out_specs, check_vma=False
    )
```

```python
import jax
import jax.numpy as jnp
from jax import lax
from jax.experimental import pallas as pl
from jax.experimental.pallas import tpu as pltpu
from jax.sharding import PartitionSpec as P

MESH = pl.DeviceIdType.MESH
STEPS = 10
ROWS = 16
COLS = 8
NB = 1024
SHARD = 64
LANES = 128
DIAG = STEPS * SHARD
PRIOR = 3712
PACKED = PRIOR // 2
HALF = PACKED // 2
SLAB = 512
SLABS = PRIOR // SLAB
TAIL = PRIOR - SLABS * SLAB
PARTS = ((0, DIAG // 2), (DIAG // 2, DIAG // 2), (DIAG, HALF), (DIAG + HALF, HALF))
STAGED = 1024
GROUPS = ((0, 1), (1, 2), (3, 7))


def split(value):
    high = value.astype(jnp.bfloat16)
    return high, (value - high.astype(jnp.float32)).astype(jnp.bfloat16)


def dot(left, right):
    return jnp.dot(left, right, preferred_element_type=jnp.float32)


def wrap(value, size=4):
    return lax.rem(value + size, size)


def kernel(
    target_ref, prior_ref, diag_ref, panel_ref, below_ref, out_ref,
    blocks, panel_high, panel_low, stage, factor, total, terms, arrived, held, own, weights, wide_high, wide_low,
    block_send, block_recv, stage_sem, factor_send, factor_recv, term_send, term_recv, send_sem, recv_sem,
):
    row = lax.axis_index("row")
    col = lax.axis_index("col")
    z, x = row // 4, lax.rem(row, 4)
    y, core = col // 2, lax.rem(col, 2)
    swap = core == 1
    first, second = jnp.where(swap, z, x), jnp.where(swap, x, z)
    chunk_of = lambda c: jnp.where(lax.rem(c, 2) == 1, 7 - c // 2, c // 2)
    mine = chunk_of(col)
    lane = lax.broadcasted_iota(jnp.int32, (1, LANES), 1)
    low_lanes = lane < 64

    def turn(value):
        return pltpu.roll(value, 64, 1)

    def panel_copy(q):
        width = min(STAGED, PRIOR - q * STAGED)
        return pltpu.make_async_copy(
            panel_ref.at[:, :, pl.ds(q * STAGED, width)], stage.at[q % 2, :, :, pl.ds(0, width)], stage_sem.at[q % 2, 0]
        )

    def below_copy(j, i):
        return pltpu.make_async_copy(
            below_ref.at[i * (i - 1) // 2 + j], stage.at[lax.rem(j, 2), i], stage_sem.at[lax.rem(j, 2), i]
        )

    panel_copy(0).start()
    panel_copy(1).start()

    barrier = pltpu.get_barrier_semaphore()
    for d in range(1, ROWS):
        pl.semaphore_signal(barrier, inc=1, device_id={"row": wrap(row + d, ROWS)}, device_id_type=MESH)
    for d in range(1, COLS):
        pl.semaphore_signal(barrier, inc=1, device_id={"col": wrap(col + d, COLS)}, device_id_type=MESH)

    lanes_of_mine = pl.ds(pl.multiple_of(mine * LANES, LANES), LANES)
    blocks[second, first, :DIAG] = diag_ref[:, :, lanes_of_mine].reshape(DIAG, LANES)
    for m in range(SLABS):
        piece = jnp.concatenate(
            [prior_ref[:, m * SLAB : m * SLAB + 256], prior_ref[:, m * SLAB + 256 : (m + 1) * SLAB]], axis=0
        )
        blocks[second, first, DIAG + 256 * m : DIAG + 256 * (m + 1)] = piece.T
    piece = prior_ref[:, SLABS * SLAB :].T
    blocks[second, first, DIAG + 256 * SLABS :] = jnp.concatenate([piece[:64], piece[64:]], axis=1)
    own[...] = target_ref[...]

    pl.semaphore_wait(barrier, ROWS + COLS - 2)

    def row_of(s, f):
        s, f = wrap(s), wrap(f)
        return jnp.where(swap, f * 4 + s, s * 4 + f)

    started = []

    def guarded(s, f, part, action):
        if part < 2:
            pl.when(row_of(s, f) >= 2 * mine)(action)
        else:
            action()

    def send(s_to, f_to, ds, df, part):
        s, f = wrap(s_to - ds), wrap(f_to - df)
        rows = pl.ds(*PARTS[part])
        copy = pltpu.make_async_remote_copy(
            src_ref=blocks.at[s, f, rows],
            dst_ref=blocks.at[s, f, rows],
            send_sem=block_send.at[len(started)],
            recv_sem=block_recv.at[wrap(ds), wrap(df), part],
            device_id={"row": row_of(s_to, f_to)},
            device_id_type=MESH,
        )
        guarded(s, f, part, copy.start)
        started.append((s, f, part, copy))

    def wait(ds, df, part):
        s, f = wrap(second - ds), wrap(first - df)
        rows = pl.ds(*PARTS[part])
        copy = pltpu.make_async_remote_copy(
            src_ref=blocks.at[s, f, rows],
            dst_ref=blocks.at[s, f, rows],
            send_sem=block_send.at[0],
            recv_sem=block_recv.at[ds, df, part],
            device_id={"row": row_of(second + 1, first)},
            device_id_type=MESH,
        )
        guarded(s, f, part, copy.wait_recv)

    def up(df, part):
        send(second + 1, first, 1, df, part)
        send(second - 1, first, 3, df, part)

    def begin(parts):
        for part in parts:
            send(second, first + 1, 0, 1, part)
            send(second, first - 1, 0, 3, part)
        for part in parts:
            up(0, part)

    def near(parts):
        for part in parts:
            wait(0, 1, part)
            if part % 2 == 0:
                send(second, first + 1, 0, 2, part)
            up(1, part)
            wait(0, 3, part)
            if part % 2 == 1:
                send(second, first - 1, 0, 2, part)
            up(3, part)

    def far(parts):
        for part in parts:
            wait(0, 2, part)
            up(2, part)

    def onward(df, parts):
        for part in parts:
            wait(1, df, part)
            wait(3, df, part)
            if part % 2 == 0:
                send(second + 1, first, 2, df, part)
            else:
                send(second - 1, first, 2, df, part)

    def last(df, parts):
        for part in parts:
            wait(2, df, part)

    begin((0, 1))
    begin((2, 3))

    for q in range(4):
        panel_copy(q).wait()
        width = min(STAGED, PRIOR - q * STAGED)
        for k in range(STEPS):
            high, low = split(stage[q % 2, k, :, :width])
            panel_high[k * SHARD : (k + 1) * SHARD, q * STAGED : q * STAGED + width] = high
            panel_low[k * SHARD : (k + 1) * SHARD, q * STAGED : q * STAGED + width] = low
        if q + 2 < 4:
            panel_copy(q + 2).start()

    def below_start(j):
        lax.fori_loop(j + 1, STEPS, lambda i, c: (below_copy(j, i).start(), c)[1], 0)

    below_start(0)
    below_start(1)

    near((0, 1))
    far((0, 1))
    near((2, 3))
    for df in (0, 1, 3, 2):
        onward(df, (0, 1))
    far((2, 3))
    for df in (0, 1, 3, 2):
        last(df, (0, 1))

    def times(block):
        high, low = split(block)
        both = dot(high, weights[...])
        return both[:, :LANES] + both[:, LANES:] + dot(low, weights[:, :LANES])

    def factor_step(j, carry):
        for r in range(ROWS):
            s, f = jnp.where(swap, r % 4, r // 4), jnp.where(swap, r // 4, r % 4)
            value = blocks[s, f, pl.ds(pl.multiple_of(j * SHARD, SHARD), SHARD)]
            high, low = split(jnp.where(r >= 2 * mine, value, 0.0))
            weights[r * SHARD : (r + 1) * SHARD, :LANES] = high
            weights[r * SHARD : (r + 1) * SHARD, LANES:] = low
        lax.fori_loop(j + 1, STEPS, lambda i, c: (below_copy(j, i).wait(), c)[1], 0)

        def three(g, carry):
            at = [jnp.minimum(j + 1 + 3 * g + t, STEPS - 1) for t in range(3)]
            result = times(jnp.concatenate([stage[lax.rem(j, 2), i] for i in at], axis=0))
            for t in range(3):
                factor[mine, at[t] * (at[t] - 1) // 2 + j] = result[t * SHARD : (t + 1) * SHARD]
            return carry

        lax.fori_loop(0, (STEPS - 1 - j + 2) // 3, three, 0)

        @pl.when(j + 2 < STEPS - 1)
        def _():
            below_start(j + 2)

        return carry

    lax.fori_loop(0, STEPS - 1, factor_step, 0)

    def factor_copy(k, source, to, half=None):
        part = factor.at[chunk_of(source)]
        if half is not None:
            part = part.at[pl.ds(half * 23, 23 - half)]
        return pltpu.make_async_remote_copy(
            src_ref=part,
            dst_ref=part,
            send_sem=factor_send.at[k],
            recv_sem=factor_recv.at[k],
            device_id={"col": to},
            device_id_type=MESH,
        )

    def side(dy, other=0):
        return wrap(y + dy) * 2 + (1 - core if other else core)

    factor_copy(1, col, side(1)).start()
    factor_copy(2, col, side(-1)).start()
    factor_copy(0, col, side(0, 1)).start()

    def slab_weights(rows_of, height):
        parts = [rows_of(f) for f in range(4)]
        turned = [turn(p) for p in parts]
        upper = [jnp.where(low_lanes, parts[f], turned[f + 1]) for f in (0, 2)]
        lower = [jnp.where(low_lanes, turned[f], parts[f + 1]) for f in (0, 2)]
        for side_at, values in ((0, upper), (height, lower)):
            for n in range(2):
                high, low = split(values[n])
                wide_high[side_at : side_at + height, n * LANES : (n + 1) * LANES] = high
                wide_low[side_at : side_at + height, n * LANES : (n + 1) * LANES] = low

    def panel_term(columns, depth):
        high = panel_high[:, columns]
        return (
            dot(high, wide_high[:depth])
            + dot(high, wide_low[:depth])
            + dot(panel_low[:, columns], wide_high[:depth])
        )

    def panel_product(s):
        def slab(m, carry):
            at = pl.multiple_of(DIAG + 256 * m, 256 if DIAG % 256 == 0 else 128)
            slab_weights(lambda f: blocks[s, f, pl.ds(at, 256)], 256)
            total[...] += panel_term(pl.ds(pl.multiple_of(m * SLAB, SLAB), SLAB), SLAB)
            return carry

        slab_weights(lambda f: blocks[s, f, DIAG + 256 * SLABS :], 64)
        total[...] = panel_term(pl.ds(SLABS * SLAB, TAIL), TAIL)
        lax.fori_loop(0, SLABS, slab, 0)

        @pl.when(core == 0)
        def _():
            for n in range(2):
                terms[2 * s + n] = total[:, n * LANES : (n + 1) * LANES].reshape(STEPS, SHARD, LANES)

        @pl.when(core == 1)
        def _():
            odd = lax.rem(s, 2)
            keep = lane // 64 == odd
            for f in range(4):
                value = total[:, (f // 2) * LANES : (f // 2 + 1) * LANES]
                value = jnp.where(odd == f % 2, value, turn(value)).reshape(STEPS, SHARD, LANES)
                at = 2 * f + s // 2
                terms[at] = jnp.where(keep.reshape(1, 1, LANES), value, terms[at])

    def term_copy(source, to, g):
        steps = pl.ds(*GROUPS[g])
        return pltpu.make_async_remote_copy(
            src_ref=terms.at[to, steps],
            dst_ref=arrived.at[source, steps],
            send_sem=term_send.at[to, g],
            recv_sem=term_recv.at[source, g],
            device_id={"col": to},
            device_id_type=MESH,
        )

    def give(targets):
        for g in range(len(GROUPS)):
            for to in targets:
                pl.when(to != col)(lambda to=to, g=g: term_copy(col, to, g).start())

    def give_zero(s):
        pl.when(core == 0)(lambda: give([2 * s, 2 * s + 1]))

    def give_one(half):
        pl.when(core == 1)(lambda: give([2 * f + half for f in range(4)]))

    panel_product(second)
    give_zero(second)
    for df in (0, 1, 3, 2):
        onward(df, (2, 3))

    factor_copy(1, side(-1), side(1)).wait_recv()
    factor_copy(3, side(-1), side(1), 0).start()
    factor_copy(5, side(-1), side(0, 1)).start()
    factor_copy(2, side(1), side(-1)).wait_recv()
    factor_copy(4, side(1), side(-1), 1).start()
    factor_copy(6, side(1), side(0, 1)).start()

    even = lax.rem(second, 2) == 0
    pair = jnp.where(even, second + 1, second - 1)
    other = wrap(pair + 2)
    panel_product(pair)
    give_zero(pair)
    give_one(second // 2)
    panel_product(other)
    give_zero(other)

    factor_copy(3, side(2), side(1), 0).wait_recv()
    factor_copy(4, side(2), side(1), 1).wait_recv()
    factor_copy(7, side(2), side(0, 1)).start()

    for df in (0, 1, 3, 2):
        last(df, (2, 3))
    panel_product(wrap(second + 2))
    give_zero(wrap(second + 2))
    give_one(1 - second // 2)

    factor_copy(0, side(0, 1), col).wait_recv()
    factor_copy(5, side(-1, 1), col).wait_recv()
    factor_copy(6, side(1, 1), col).wait_recv()
    factor_copy(7, side(2, 1), col).wait_recv()

    def ready(g):
        begin_at, count = GROUPS[g]
        for d in range(1, COLS):
            term_copy(wrap(col + d, COLS), col, g).wait_recv()
        for k in range(begin_at, begin_at + count):
            value = terms[col, k]
            for d in range(1, COLS):
                value = value + arrived[wrap(col + d, COLS), k]
            own[k] -= value

    def copy(k, d):
        slot = lax.rem(k, 2)
        return pltpu.make_async_remote_copy(
            src_ref=own.at[k],
            dst_ref=held.at[slot, row],
            send_sem=send_sem.at[slot, d],
            recv_sem=recv_sem.at[slot, d],
            device_id={"row": wrap(row + d, ROWS)},
            device_id_type=MESH,
        )

    def spread(k):
        for d in range(1, ROWS):
            copy(k, d).start()
        held[lax.rem(k, 2), row] = own[k]

    def arrive(k):
        for d in range(1, ROWS):
            copy(k, d).wait_recv()
        high, low = split(held[lax.rem(k, 2)].reshape(NB, LANES))
        weights[...] = jnp.concatenate([high, low], axis=1)

    def coupling(i, k):
        at = i * (i - 1) // 2 + k
        return jnp.concatenate([factor[c, at] for c in range(COLS)], axis=1)

    ready(0)
    spread(0)

    def step(k, carry):
        @pl.when(k == 0)
        def _():
            ready(1)

        @pl.when(k == 2)
        def _():
            ready(2)

        arrive(k)
        own[k + 1] -= times(coupling(k + 1, k))
        spread(k + 1)
        out_ref[k] = times(diag_ref[k])

        def later(i, carry):
            own[i] -= times(coupling(i, k))
            return carry

        lax.fori_loop(k + 2, STEPS, later, 0)
        for d in range(1, ROWS):
            copy(k, d).wait_send()
        return carry

    lax.fori_loop(0, STEPS - 1, step, 0)
    arrive(STEPS - 1)
    out_ref[STEPS - 1] = times(diag_ref[STEPS - 1])

    for d in range(1, ROWS):
        copy(STEPS - 1, d).wait_send()
    for s, f, part, sent in started:
        guarded(s, f, part, sent.wait_send)
    for k, half in enumerate((None, None, None, 0, 1, None, None, None)):
        factor_copy(k, col, side(1), half).wait_send()
    for g in range(len(GROUPS)):
        for d in range(1, COLS):
            term_copy(col, wrap(col + d, COLS), g).wait_send()


def on_device(targets, lower_panel, prior_solution, diag_inverse, below_blocks):
    f32, bf16 = jnp.float32, jnp.bfloat16
    vmem = pl.BlockSpec(memory_space=pltpu.VMEM)
    hbm = pl.BlockSpec(memory_space=pl.ANY)
    dma = pltpu.SemaphoreType.DMA
    return pl.pallas_call(
        kernel,
        out_shape=jax.ShapeDtypeStruct(targets.shape, f32),
        in_specs=[vmem, vmem, vmem, hbm, hbm],
        out_specs=vmem,
        scratch_shapes=[
            pltpu.VMEM((4, 4, DIAG + PACKED, LANES), f32),
            pltpu.VMEM((DIAG, PRIOR), bf16),
            pltpu.VMEM((DIAG, PRIOR), bf16),
            pltpu.VMEM((2, STEPS, SHARD, STAGED), f32),
            pltpu.VMEM((COLS, STEPS * (STEPS - 1) // 2, SHARD, LANES), f32),
            pltpu.VMEM((DIAG, 2 * LANES), f32),
            pltpu.VMEM((COLS, STEPS, SHARD, LANES), f32),
            pltpu.VMEM((COLS, STEPS, SHARD, LANES), f32),
            pltpu.VMEM((2, ROWS, SHARD, LANES), f32),
            pltpu.VMEM((STEPS, SHARD, LANES), f32),
            pltpu.VMEM((NB, 2 * LANES), bf16),
            pltpu.VMEM((SLAB, 2 * LANES), bf16),
            pltpu.VMEM((SLAB, 2 * LANES), bf16),
            dma((64,)),
            dma((4, 4, 4)),
            dma((2, STEPS)),
            dma((8,)),
            dma((8,)),
            dma((COLS, len(GROUPS))),
            dma((COLS, len(GROUPS))),
            dma((2, ROWS)),
            dma((2, ROWS)),
        ],
        compiler_params=pltpu.CompilerParams(collective_id=0, has_side_effects=True, vmem_limit_bytes=63 << 20),
    )(targets, prior_solution.T, diag_inverse, lower_panel, below_blocks)


def solution(mesh):
    in_specs = (
        P(None, "row", "col"),
        P(None, "row", "col"),
        P("col", "row"),
        P(None, "row", None),
        P(None, "row", None),
    )
    out_specs = P(None, "row", "col")
    return jax.shard_map(
        on_device, mesh=mesh, in_specs=in_specs, out_specs=out_specs, check_vma=False
    )
```

```python
import jax
import jax.numpy as jnp
from jax import lax
from jax.experimental import pallas as pl
from jax.experimental.pallas import tpu as pltpu
from jax.sharding import PartitionSpec as P

MESH = pl.DeviceIdType.MESH
STEPS = 10
ROWS = 16
COLS = 8
NB = 1024
SHARD = 64
LANES = 128
DIAG = STEPS * SHARD
PRIOR = 3712
PACKED = PRIOR // 2
SLAB = 512
SLABS = PRIOR // SLAB
TAIL = PRIOR - SLABS * SLAB
TAKEN = (STEPS // 2) * SHARD
EARLY = 1024
LATE = PACKED - EARLY
PARTS = tuple((n * TAKEN // 2, TAKEN // 2) for n in range(4)) + (
    (DIAG, EARLY // 2),
    (DIAG + EARLY // 2, EARLY // 2),
    (DIAG + EARLY, LATE // 2),
    (DIAG + EARLY + LATE // 2, LATE // 2),
)
SMALL, FRONT, BACK = (0, 1, 2, 3), (4, 5), (6, 7)
ORDER = (0, 1, 3, 2)
PEERS = (10, 6, 14, 9, 11, 5, 15, 7, 13, 8, 2, 4, 1, 12, 3)
PAIRS = STEPS * (STEPS - 1) // 2
STAGED = 1024
GROUPS = ((0, 1), (1, 2), (3, 7))


def split(value):
    high = value.astype(jnp.bfloat16)
    return high, (value - high.astype(jnp.float32)).astype(jnp.bfloat16)


def dot(left, right):
    return jnp.dot(left, right, preferred_element_type=jnp.float32)


def pairs_of(j):
    return (STEPS - 1) * j - j * (j - 1) // 2, STEPS - 1 - j


def wrap(value, size=4):
    return lax.rem(value + size, size)


def kernel(
    target_ref, prior_ref, diag_ref, panel_ref, below_ref, out_ref,
    blocks, panel_high, panel_low, stage, factor, total, terms, arrived, held, own, weights, wide_high, wide_low,
    block_send, block_recv, stage_sem, factor_send, factor_recv, term_send, term_recv, send_sem, recv_sem,
):
    row = lax.axis_index("row")
    col = lax.axis_index("col")
    z, x = row // 4, lax.rem(row, 4)
    y, core = col // 2, lax.rem(col, 2)
    swap = core == 1
    second = jnp.where(swap, x, z)
    groups = (y, 7 - y)
    lane = lax.broadcasted_iota(jnp.int32, (1, LANES), 1)
    low_lanes = lane < 64

    def turn(value):
        return pltpu.roll(value, 64, 1)

    def panel_copy(q):
        width = min(STAGED, PRIOR - q * STAGED)
        return pltpu.make_async_copy(
            panel_ref.at[:, :, pl.ds(q * STAGED, width)], stage.at[q % 2, :, :, pl.ds(0, width)], stage_sem.at[q % 2, 0]
        )

    def below_copy(j, i):
        slot = j // 2 % 2
        return pltpu.make_async_copy(below_ref.at[i * (i - 1) // 2 + j], stage.at[slot, i], stage_sem.at[slot, i])

    panel_copy(0).start()
    panel_copy(1).start()

    barrier = pltpu.get_barrier_semaphore()
    for d in range(1, ROWS):
        pl.semaphore_signal(barrier, inc=1, device_id={"row": wrap(row + d, ROWS)}, device_id_type=MESH)
    for d in range(1, COLS):
        pl.semaphore_signal(barrier, inc=1, device_id={"col": wrap(col + d, COLS)}, device_id_type=MESH)

    for n in range(2):
        lanes = pl.ds(pl.multiple_of(groups[n] * LANES, LANES), LANES)
        for t in range(STEPS // 2):
            blocks[row, n * TAKEN + t * SHARD : n * TAKEN + (t + 1) * SHARD] = diag_ref[2 * t + core, :, lanes]
    for m in range(SLABS):
        piece = jnp.concatenate(
            [prior_ref[:, m * SLAB : m * SLAB + 256], prior_ref[:, m * SLAB + 256 : (m + 1) * SLAB]], axis=0
        )
        blocks[row, DIAG + 256 * m : DIAG + 256 * (m + 1)] = piece.T
    piece = prior_ref[:, SLABS * SLAB :].T
    blocks[row, DIAG + 256 * SLABS :] = jnp.concatenate([piece[:64], piece[64:]], axis=1)
    own[...] = target_ref[...]

    pl.semaphore_wait(barrier, ROWS + COLS - 2)

    def turned_of(part):
        return jnp.bool_(True) if part in (2, 3) else swap

    def place(part):
        turned = turned_of(part)
        return jnp.where(turned, x, z), jnp.where(turned, z, x)

    def row_of(part, s, f):
        s, f = wrap(s), wrap(f)
        return jnp.where(turned_of(part), f * 4 + s, s * 4 + f)

    started = []

    def guarded(source, part, action):
        if part in SMALL:
            pl.when(source >= 2 * groups[part // 2])(action)
        else:
            action()

    def send(part, to_s, to_f, ds, df):
        s, f = place(part)
        source = row_of(part, s + to_s - ds, f + to_f - df)
        piece = blocks.at[source, pl.ds(*PARTS[part])]
        copy = pltpu.make_async_remote_copy(
            src_ref=piece,
            dst_ref=piece,
            send_sem=block_send.at[len(started)],
            recv_sem=block_recv.at[ds, df, part],
            device_id={"row": row_of(part, s + to_s, f + to_f)},
            device_id_type=MESH,
        )
        guarded(source, part, copy.start)
        started.append((source, part, copy))

    def wait(part, ds, df):
        s, f = place(part)
        source = row_of(part, s - ds, f - df)
        piece = blocks.at[source, pl.ds(*PARTS[part])]
        copy = pltpu.make_async_remote_copy(
            src_ref=piece,
            dst_ref=piece,
            send_sem=block_send.at[0],
            recv_sem=block_recv.at[ds, df, part],
            device_id={"row": row_of(part, s + 1, f)},
            device_id_type=MESH,
        )
        guarded(source, part, copy.wait_recv)

    def up(df, part):
        send(part, 1, 0, 1, df)
        send(part, -1, 0, 3, df)

    def begin(parts):
        for part in parts:
            send(part, 0, 1, 0, 1)
            send(part, 0, -1, 0, 3)
            up(0, part)

    def near(parts):
        for part in parts:
            wait(part, 0, 1)
            if part % 2 == 0:
                send(part, 0, 1, 0, 2)
            up(1, part)
            wait(part, 0, 3)
            if part % 2 == 1:
                send(part, 0, -1, 0, 2)
            up(3, part)

    def far(parts):
        for part in parts:
            wait(part, 0, 2)
            up(2, part)

    def onward(df, parts):
        for part in parts:
            wait(part, 1, df)
            wait(part, 3, df)
            if part % 2 == 0:
                send(part, 1, 0, 2, df)
            else:
                send(part, -1, 0, 2, df)

    def last(df, parts):
        for part in parts:
            wait(part, 2, df)

    begin(SMALL)

    def convert(q):
        panel_copy(q).wait()
        width = min(STAGED, PRIOR - q * STAGED)
        for k in range(STEPS):
            high, low = split(stage[q % 2, k, :, :width])
            panel_high[k * SHARD : (k + 1) * SHARD, q * STAGED : q * STAGED + width] = high
            panel_low[k * SHARD : (k + 1) * SHARD, q * STAGED : q * STAGED + width] = low
        if q + 2 < 4:
            panel_copy(q + 2).start()

    convert(0)
    convert(1)
    near(SMALL)
    far(SMALL)
    begin(FRONT)
    begin(BACK)
    convert(2)
    convert(3)

    def below_start(j):
        for i in range(j + 1, STEPS):
            below_copy(j, i).start()

    def on_own(j, action):
        if j < STEPS - 1:
            pl.when(core == j % 2)(lambda: action(j))

    for j in range(4):
        on_own(j, below_start)

    for df in ORDER:
        onward(df, SMALL)
    near(FRONT)
    for df in ORDER:
        last(df, SMALL)
    near(BACK)

    def factor_copy(j, way, source, to):
        at, count = pairs_of(j)
        part = factor.at[source, pl.ds(at, count)]
        return pltpu.make_async_remote_copy(
            src_ref=part,
            dst_ref=part,
            send_sem=factor_send.at[j, way],
            recv_sem=factor_recv.at[j, way],
            device_id={"col": to},
            device_id_type=MESH,
        )

    def at_y(dy):
        return wrap(y + dy)

    same = lambda dy: at_y(dy) * 2 + core
    partner = y * 2 + 1 - core

    def make_factor(j):
        t = j // 2
        for n in range(2):
            for r in range(ROWS):
                value = blocks[r, n * TAKEN + t * SHARD : n * TAKEN + (t + 1) * SHARD]
                high, low = split(jnp.where(r >= 2 * groups[n], value, 0.0))
                wide_high[r * SHARD : (r + 1) * SHARD, n * LANES : (n + 1) * LANES] = high
                wide_low[r * SHARD : (r + 1) * SHARD, n * LANES : (n + 1) * LANES] = low
        at, count = pairs_of(j)
        for i in range(j + 1, STEPS):
            below_copy(j, i).wait()
        for begin_at in range(0, count, 3):
            n = min(3, count - begin_at)
            i = j + 1 + begin_at
            high, low = split(stage[t % 2, i : i + n].reshape(n * SHARD, NB))
            result = dot(high, wide_high[...]) + dot(high, wide_low[...]) + dot(low, wide_high[...])
            factor[y, at + begin_at : at + begin_at + n] = result.reshape(n, SHARD, 2 * LANES)
        if j + 4 < STEPS - 1:
            below_start(j + 4)
        factor_copy(j, 1, y, same(1)).start()
        factor_copy(j, 2, y, same(-1)).start()
        factor_copy(j, 0, y, partner).start()

    for j in range(STEPS - 1):
        on_own(j, make_factor)

    def up_goes(j):
        return j // 2 % 2 == 0

    def hop(j):
        way, dy = (1, -1) if up_goes(j) else (2, 1)
        factor_copy(j, way, at_y(dy), same(-dy)).wait_recv()
        factor_copy(j, 3, at_y(dy), same(-dy)).start()
        factor_copy(j, 3 + way, at_y(dy), partner).start()

    def pass_on(j):
        way, dy = (2, 1) if up_goes(j) else (1, -1)
        factor_copy(j, way, at_y(dy), same(1)).wait_recv()
        factor_copy(j, 3 + way, at_y(dy), partner).start()
        factor_copy(j, 3, at_y(2), same(1)).wait_recv()
        factor_copy(j, 6, at_y(2), partner).start()

    def need(j):
        @pl.when(core != j % 2)
        def _():
            for way, dy in ((0, 0), (4, -1), (5, 1), (6, 2)):
                factor_copy(j, way, at_y(dy), partner).wait_recv()

    def slab_weights(rows_of, height):
        parts = [rows_of(f) for f in range(4)]
        turned = [turn(p) for p in parts]
        upper = [jnp.where(low_lanes, parts[f], turned[f + 1]) for f in (0, 2)]
        lower = [jnp.where(low_lanes, turned[f], parts[f + 1]) for f in (0, 2)]
        for side_at, values in ((0, upper), (height, lower)):
            for n in range(2):
                high, low = split(values[n])
                wide_high[side_at : side_at + height, n * LANES : (n + 1) * LANES] = high
                wide_low[side_at : side_at + height, n * LANES : (n + 1) * LANES] = low

    def panel_term(columns, depth):
        high = panel_high[:, columns]
        return (
            dot(high, wide_high[:depth])
            + dot(high, wide_low[:depth])
            + dot(panel_low[:, columns], wide_high[:depth])
        )

    def group_row(s, f):
        return jnp.where(swap, f * 4 + s, s * 4 + f)

    def panel_half(s, back):
        def slab(m, carry):
            at = pl.multiple_of(DIAG + 256 * m, LANES)
            slab_weights(lambda f: blocks[group_row(s, f), pl.ds(at, 256)], 256)
            total[...] += panel_term(pl.ds(pl.multiple_of(m * SLAB, SLAB), SLAB), SLAB)
            return carry

        if back:
            slab_weights(lambda f: blocks[group_row(s, f), DIAG + 256 * SLABS :], 64)
            total[...] += panel_term(pl.ds(SLABS * SLAB, TAIL), TAIL)
            lax.fori_loop(EARLY // 256, SLABS, slab, 0)
        else:
            total[...] = jnp.zeros_like(total)
            lax.fori_loop(0, EARLY // 256, slab, 0)

    def keep_terms(s):
        @pl.when(core == 0)
        def _():
            for n in range(2):
                terms[2 * s + n] = total[:, n * LANES : (n + 1) * LANES].reshape(STEPS, SHARD, LANES)

        @pl.when(core == 1)
        def _():
            odd = lax.rem(s, 2)
            keep = lane // 64 == odd
            for f in range(4):
                value = total[:, (f // 2) * LANES : (f // 2 + 1) * LANES]
                value = jnp.where(odd == f % 2, value, turn(value)).reshape(STEPS, SHARD, LANES)
                at = 2 * f + s // 2
                terms[at] = jnp.where(keep.reshape(1, 1, LANES), value, terms[at])

    def panel_product(s):
        panel_half(s, False)
        panel_half(s, True)
        keep_terms(s)

    def term_copy(source, to, g):
        steps = pl.ds(*GROUPS[g])
        return pltpu.make_async_remote_copy(
            src_ref=terms.at[to, steps],
            dst_ref=arrived.at[source, steps],
            send_sem=term_send.at[to, g],
            recv_sem=term_recv.at[source, g],
            device_id={"col": to},
            device_id_type=MESH,
        )

    def give(targets):
        for g in range(len(GROUPS)):
            for to in targets:
                pl.when(to != col)(lambda to=to, g=g: term_copy(col, to, g).start())

    def give_zero(s):
        pl.when(core == 0)(lambda: give([2 * s, 2 * s + 1]))

    def give_one(half):
        pl.when(core == 1)(lambda: give([2 * f + half for f in range(4)]))

    far(FRONT)
    far(BACK)
    panel_product(second)
    give_zero(second)
    for df, parts in ((0, FRONT), (1, FRONT), (3, FRONT), (0, BACK), (1, BACK), (3, BACK), (2, FRONT), (2, BACK)):
        onward(df, parts)

    even = lax.rem(second, 2) == 0
    pair = jnp.where(even, second + 1, second - 1)
    other = wrap(pair + 2)
    panel_product(pair)
    give_zero(pair)
    give_one(second // 2)
    for j in range(2):
        on_own(j, hop)
    panel_product(other)
    give_zero(other)
    for j in range(2, STEPS - 1):
        on_own(j, hop)
    for df in ORDER:
        last(df, FRONT)
    panel_half(wrap(second + 2), False)
    for j in range(2):
        on_own(j, pass_on)
    for df in ORDER:
        last(df, BACK)
    panel_half(wrap(second + 2), True)
    keep_terms(wrap(second + 2))
    give_zero(wrap(second + 2))
    give_one(1 - second // 2)

    def ready(g):
        begin_at, count = GROUPS[g]
        for d in range(1, COLS):
            term_copy(wrap(col + d, COLS), col, g).wait_recv()
        for k in range(begin_at, begin_at + count):
            value = terms[col, k]
            for d in range(1, COLS):
                value = value + arrived[wrap(col + d, COLS), k]
            own[k] -= value

    def copy(k, d):
        slot = k % 2
        return pltpu.make_async_remote_copy(
            src_ref=own.at[k],
            dst_ref=held.at[slot, row],
            send_sem=send_sem.at[slot, d],
            recv_sem=recv_sem.at[slot, d],
            device_id={"row": wrap(row + d, ROWS)},
            device_id_type=MESH,
        )

    def spread(k):
        for d in PEERS:
            copy(k, d).start()
        held[k % 2, row] = own[k]

    def arrive(k):
        for d in range(1, ROWS):
            copy(k, d).wait_recv()
        high, low = split(held[k % 2].reshape(NB, LANES))
        weights[...] = jnp.concatenate([high, low], axis=1)

    def times(block):
        high, low = split(block)
        both = dot(high, weights[...])
        return both[:, :LANES] + both[:, LANES:] + dot(low, weights[:, :LANES])

    def coupling(k, begin_at, end_at):
        at, _ = pairs_of(k)
        rows = slice(at + begin_at, at + end_at)
        parts = [factor[c, rows, :, :LANES] for c in range(4)] + [factor[c, rows, :, LANES:] for c in (3, 2, 1, 0)]
        return jnp.concatenate([p.reshape(-1, LANES) for p in parts], axis=1)

    ready(0)
    spread(0)
    for k in range(STEPS - 1):
        if k == 0:
            ready(1)
        if k == 2:
            ready(2)
        need(k)
        arrive(k)
        own[k + 1] -= times(coupling(k, 0, 1))
        spread(k + 1)
        if k + 2 < STEPS - 1:
            on_own(k + 2, pass_on)
        out_ref[k] = times(diag_ref[k])
        for i in range(k + 2, STEPS, 3):
            end_at = min(i + 3, STEPS)
            result = times(coupling(k, i - k - 1, end_at - k - 1))
            own[i:end_at] -= result.reshape(end_at - i, SHARD, LANES)
        for d in range(1, ROWS):
            copy(k, d).wait_send()
    arrive(STEPS - 1)
    out_ref[STEPS - 1] = times(diag_ref[STEPS - 1])

    for d in range(1, ROWS):
        copy(STEPS - 1, d).wait_send()
    for source, part, sent in started:
        guarded(source, part, sent.wait_send)
    for j in range(STEPS - 1):
        on_own(j, lambda j: [factor_copy(j, way, y, partner).wait_send() for way in range(7)] and None)
    for g in range(len(GROUPS)):
        for d in range(1, COLS):
            term_copy(col, wrap(col + d, COLS), g).wait_send()


def on_device(targets, lower_panel, prior_solution, diag_inverse, below_blocks):
    f32, bf16 = jnp.float32, jnp.bfloat16
    vmem = pl.BlockSpec(memory_space=pltpu.VMEM)
    hbm = pl.BlockSpec(memory_space=pl.ANY)
    dma = pltpu.SemaphoreType.DMA
    return pl.pallas_call(
        kernel,
        out_shape=jax.ShapeDtypeStruct(targets.shape, f32),
        in_specs=[vmem, vmem, vmem, hbm, hbm],
        out_specs=vmem,
        scratch_shapes=[
            pltpu.VMEM((ROWS, DIAG + PACKED, LANES), f32),
            pltpu.VMEM((DIAG, PRIOR), bf16),
            pltpu.VMEM((DIAG, PRIOR), bf16),
            pltpu.VMEM((2, STEPS, SHARD, STAGED), f32),
            pltpu.VMEM((4, PAIRS, SHARD, 2 * LANES), f32),
            pltpu.VMEM((DIAG, 2 * LANES), f32),
            pltpu.VMEM((COLS, STEPS, SHARD, LANES), f32),
            pltpu.VMEM((COLS, STEPS, SHARD, LANES), f32),
            pltpu.VMEM((2, ROWS, SHARD, LANES), f32),
            pltpu.VMEM((STEPS, SHARD, LANES), f32),
            pltpu.VMEM((NB, 2 * LANES), bf16),
            pltpu.VMEM((NB, 2 * LANES), bf16),
            pltpu.VMEM((NB, 2 * LANES), bf16),
            dma((15 * len(PARTS),)),
            dma((4, 4, len(PARTS))),
            dma((2, STEPS)),
            dma((STEPS - 1, 7)),
            dma((STEPS - 1, 7)),
            dma((COLS, len(GROUPS))),
            dma((COLS, len(GROUPS))),
            dma((2, ROWS)),
            dma((2, ROWS)),
        ],
        compiler_params=pltpu.CompilerParams(collective_id=0, has_side_effects=True, vmem_limit_bytes=63 << 20),
    )(targets, prior_solution.T, diag_inverse, lower_panel, below_blocks)


def solution(mesh):
    in_specs = (
        P(None, "row", "col"),
        P(None, "row", "col"),
        P("col", "row"),
        P(None, "row", None),
        P(None, "row", None),
    )
    out_specs = P(None, "row", "col")
    return jax.shard_map(
        on_device, mesh=mesh, in_specs=in_specs, out_specs=out_specs, check_vma=False
    )
```

```python
import jax
import jax.numpy as jnp
from jax import lax
from jax.experimental import pallas as pl
from jax.experimental.pallas import tpu as pltpu
from jax.sharding import PartitionSpec as P

MESH = pl.DeviceIdType.MESH
STEPS = 10
ROWS = 16
COLS = 8
NB = 1024
SHARD = 64
LANES = 128
DIAG = STEPS * SHARD
PRIOR = 3712
PACKED = PRIOR // 2
SLAB = 512
SLABS = PRIOR // SLAB
TAIL = PRIOR - SLABS * SLAB
TAKEN = (STEPS // 2) * SHARD
EARLY = 1024
LATE = PACKED - EARLY
PARTS = (
    (0, 128),
    (128, 128),
    (256, 64),
    (TAKEN, 128),
    (TAKEN + 128, 128),
    (TAKEN + 256, 64),
    (DIAG, EARLY // 2),
    (DIAG + EARLY // 2, EARLY // 2),
    (DIAG + EARLY, LATE // 2),
    (DIAG + EARLY + LATE // 2, LATE // 2),
)
SMALL, FRONT, BACK = (0, 1, 2, 3, 4, 5), (6, 7), (8, 9)
ORDER = (0, 1, 3, 2)
PEERS = (10, 6, 14, 9, 11, 5, 15, 7, 13, 8, 2, 4, 1, 12, 3)
PAIRS = STEPS * (STEPS - 1) // 2
STAGED = 1024
GROUPS = ((0, 1), (1, 2), (3, 3), (6, 4))
AHEAD = 4


def split(value):
    high = value.astype(jnp.bfloat16)
    return high, (value - high.astype(jnp.float32)).astype(jnp.bfloat16)


def dot(left, right):
    return jnp.dot(left, right, preferred_element_type=jnp.float32)


def pairs_of(j):
    return (STEPS - 1) * j - j * (j - 1) // 2, STEPS - 1 - j


def wrap(value, size=4):
    return lax.rem(value + size, size)


def kernel(
    target_ref, prior_ref, diag_ref, panel_ref, below_ref, out_ref,
    blocks, panel_high, panel_low, stage, factor, total, terms, arrived, held, own, weights, wide_high, wide_low,
    block_send, block_recv, stage_sem, factor_send, factor_recv, term_send, term_recv, send_sem, recv_sem,
):
    row = lax.axis_index("row")
    col = lax.axis_index("col")
    z, x = row // 4, lax.rem(row, 4)
    y, core = col // 2, lax.rem(col, 2)
    swap = core == 1
    second = jnp.where(swap, x, z)
    groups = (y, 7 - y)
    lane = lax.broadcasted_iota(jnp.int32, (1, LANES), 1)
    low_lanes = lane < 64

    def turn(value):
        return pltpu.roll(value, 64, 1)

    def panel_copy(q):
        width = min(STAGED, PRIOR - q * STAGED)
        return pltpu.make_async_copy(
            panel_ref.at[:, :, pl.ds(q * STAGED, width)], stage.at[q % 2, :, :, pl.ds(0, width)], stage_sem.at[q % 2, 0]
        )

    def below_copy(j, i):
        slot = j // 2 % 2
        return pltpu.make_async_copy(below_ref.at[i * (i - 1) // 2 + j], stage.at[slot, i], stage_sem.at[slot, i])

    panel_copy(0).start()
    panel_copy(1).start()

    barrier = pltpu.get_barrier_semaphore()
    for d in range(1, ROWS):
        pl.semaphore_signal(barrier, inc=1, device_id={"row": wrap(row + d, ROWS)}, device_id_type=MESH)
    for d in range(1, COLS):
        pl.semaphore_signal(barrier, inc=1, device_id={"col": wrap(col + d, COLS)}, device_id_type=MESH)

    for n in range(2):
        lanes = pl.ds(pl.multiple_of(groups[n] * LANES, LANES), LANES)
        for t in range(STEPS // 2):
            blocks[row, n * TAKEN + t * SHARD : n * TAKEN + (t + 1) * SHARD] = diag_ref[2 * t + core, :, lanes]
    for m in range(SLABS):
        piece = jnp.concatenate(
            [prior_ref[:, m * SLAB : m * SLAB + 256], prior_ref[:, m * SLAB + 256 : (m + 1) * SLAB]], axis=0
        )
        blocks[row, DIAG + 256 * m : DIAG + 256 * (m + 1)] = piece.T
    piece = prior_ref[:, SLABS * SLAB :].T
    blocks[row, DIAG + 256 * SLABS :] = jnp.concatenate([piece[:64], piece[64:]], axis=1)
    own[...] = target_ref[...]

    pl.semaphore_wait(barrier, ROWS + COLS - 2)

    def turned_of(part):
        return jnp.bool_(True) if part in (3, 4, 5) else swap

    def place(part):
        turned = turned_of(part)
        return jnp.where(turned, x, z), jnp.where(turned, z, x)

    def row_of(part, s, f):
        s, f = wrap(s), wrap(f)
        return jnp.where(turned_of(part), f * 4 + s, s * 4 + f)

    started = []

    def guarded(source, part, action):
        if part in SMALL:
            needed = source >= 2 * groups[part // 3]
            pl.when(jnp.logical_and(needed, core == 0) if part in (2, 5) else needed)(action)
        else:
            action()

    def send(part, to_s, to_f, ds, df):
        s, f = place(part)
        source = row_of(part, s + to_s - ds, f + to_f - df)
        piece = blocks.at[source, pl.ds(*PARTS[part])]
        copy = pltpu.make_async_remote_copy(
            src_ref=piece,
            dst_ref=piece,
            send_sem=block_send.at[len(started)],
            recv_sem=block_recv.at[ds, df, part],
            device_id={"row": row_of(part, s + to_s, f + to_f)},
            device_id_type=MESH,
        )
        guarded(source, part, copy.start)
        started.append((source, part, copy))

    def wait(part, ds, df):
        s, f = place(part)
        source = row_of(part, s - ds, f - df)
        piece = blocks.at[source, pl.ds(*PARTS[part])]
        copy = pltpu.make_async_remote_copy(
            src_ref=piece,
            dst_ref=piece,
            send_sem=block_send.at[0],
            recv_sem=block_recv.at[ds, df, part],
            device_id={"row": row_of(part, s + 1, f)},
            device_id_type=MESH,
        )
        guarded(source, part, copy.wait_recv)

    def up(df, part):
        send(part, 1, 0, 1, df)
        send(part, -1, 0, 3, df)

    def begin(parts):
        for part in parts:
            send(part, 0, 1, 0, 1)
            send(part, 0, -1, 0, 3)
            up(0, part)

    def near(parts):
        for part in parts:
            wait(part, 0, 1)
            if part % 2 == 0:
                send(part, 0, 1, 0, 2)
            up(1, part)
            wait(part, 0, 3)
            if part % 2 == 1:
                send(part, 0, -1, 0, 2)
            up(3, part)

    def far(parts):
        for part in parts:
            wait(part, 0, 2)
            up(2, part)

    def onward(df, parts):
        for part in parts:
            wait(part, 1, df)
            wait(part, 3, df)
            if part % 2 == 0:
                send(part, 1, 0, 2, df)
            else:
                send(part, -1, 0, 2, df)

    def last(df, parts):
        for part in parts:
            wait(part, 2, df)

    begin(SMALL)

    def convert(q):
        panel_copy(q).wait()
        width = min(STAGED, PRIOR - q * STAGED)
        for k in range(STEPS):
            high, low = split(stage[q % 2, k, :, :width])
            panel_high[k * SHARD : (k + 1) * SHARD, q * STAGED : q * STAGED + width] = high
            panel_low[k * SHARD : (k + 1) * SHARD, q * STAGED : q * STAGED + width] = low
        if q + 2 < 4:
            panel_copy(q + 2).start()

    convert(0)
    convert(1)
    near(SMALL)
    far(SMALL)
    begin(FRONT)
    begin(BACK)
    convert(2)
    convert(3)

    def below_start(j):
        for i in range(j + 1, STEPS):
            below_copy(j, i).start()

    def on_own(j, action):
        if j < STEPS - 1:
            pl.when(core == j % 2)(lambda: action(j))

    for j in range(4):
        on_own(j, below_start)

    for df in ORDER:
        onward(df, SMALL)
    near(FRONT)
    for df in ORDER:
        last(df, SMALL)

    def factor_copy(j, way, source, to):
        at, count = pairs_of(j)
        part = factor.at[source, pl.ds(at, count)]
        return pltpu.make_async_remote_copy(
            src_ref=part,
            dst_ref=part,
            send_sem=factor_send.at[j, way],
            recv_sem=factor_recv.at[j, way],
            device_id={"col": to},
            device_id_type=MESH,
        )

    def at_y(dy):
        return wrap(y + dy)

    same = lambda dy: at_y(dy) * 2 + core
    partner = y * 2 + 1 - core

    def share(j):
        factor_copy(j, 1, y, same(1)).start()
        factor_copy(j, 2, y, same(-1)).start()
        factor_copy(j, 0, y, partner).start()

    def make_factor(j):
        t = j // 2
        for n in range(2):
            for r in range(ROWS):
                value = blocks[r, n * TAKEN + t * SHARD : n * TAKEN + (t + 1) * SHARD]
                high, low = split(jnp.where(r >= 2 * groups[n], value, 0.0))
                wide_high[r * SHARD : (r + 1) * SHARD, n * LANES : (n + 1) * LANES] = high
                wide_low[r * SHARD : (r + 1) * SHARD, n * LANES : (n + 1) * LANES] = low
        at, count = pairs_of(j)
        for i in range(j + 1, STEPS):
            below_copy(j, i).wait()
        for begin_at in range(0, count, 3):
            n = min(3, count - begin_at)
            i = j + 1 + begin_at
            high, low = split(stage[t % 2, i : i + n].reshape(n * SHARD, NB))
            result = dot(high, wide_high[...]) + dot(high, wide_low[...]) + dot(low, wide_high[...])
            factor[y, at + begin_at : at + begin_at + n] = result.reshape(n, SHARD, 2 * LANES)
        if j + 4 < STEPS - 1:
            below_start(j + 4)
        if j < AHEAD:
            share(j)

    for j in range(STEPS - 1):
        on_own(j, make_factor)
    near(BACK)

    def up_goes(j):
        return j // 2 % 2 == 0

    def hop(j):
        way, dy = (1, -1) if up_goes(j) else (2, 1)
        factor_copy(j, way, at_y(dy), same(-dy)).wait_recv()
        factor_copy(j, 3, at_y(dy), same(-dy)).start()
        factor_copy(j, 3 + way, at_y(dy), partner).start()

    def pass_on(j):
        way, dy = (2, 1) if up_goes(j) else (1, -1)
        factor_copy(j, way, at_y(dy), same(1)).wait_recv()
        factor_copy(j, 3 + way, at_y(dy), partner).start()
        factor_copy(j, 3, at_y(2), same(1)).wait_recv()
        factor_copy(j, 6, at_y(2), partner).start()

    def need(j):
        @pl.when(core != j % 2)
        def _():
            for way, dy in ((0, 0), (4, -1), (5, 1), (6, 2)):
                factor_copy(j, way, at_y(dy), partner).wait_recv()

    def slab_weights(rows_of, height):
        parts = [rows_of(f) for f in range(4)]
        turned = [turn(p) for p in parts]
        upper = [jnp.where(low_lanes, parts[f], turned[f + 1]) for f in (0, 2)]
        lower = [jnp.where(low_lanes, turned[f], parts[f + 1]) for f in (0, 2)]
        for side_at, values in ((0, upper), (height, lower)):
            for n in range(2):
                high, low = split(values[n])
                wide_high[side_at : side_at + height, n * LANES : (n + 1) * LANES] = high
                wide_low[side_at : side_at + height, n * LANES : (n + 1) * LANES] = low

    def panel_term(columns, depth):
        high = panel_high[:, columns]
        return (
            dot(high, wide_high[:depth])
            + dot(high, wide_low[:depth])
            + dot(panel_low[:, columns], wide_high[:depth])
        )

    def group_row(s, f):
        return jnp.where(swap, f * 4 + s, s * 4 + f)

    def panel_half(s, back):
        def slab(m, carry):
            at = pl.multiple_of(DIAG + 256 * m, LANES)
            slab_weights(lambda f: blocks[group_row(s, f), pl.ds(at, 256)], 256)
            total[...] += panel_term(pl.ds(pl.multiple_of(m * SLAB, SLAB), SLAB), SLAB)
            return carry

        if back:
            slab_weights(lambda f: blocks[group_row(s, f), DIAG + 256 * SLABS :], 64)
            total[...] += panel_term(pl.ds(SLABS * SLAB, TAIL), TAIL)
            lax.fori_loop(EARLY // 256, SLABS, slab, 0)
        else:
            total[...] = jnp.zeros_like(total)
            lax.fori_loop(0, EARLY // 256, slab, 0)

    def keep_terms(s):
        @pl.when(core == 0)
        def _():
            for n in range(2):
                terms[2 * s + n] = total[:, n * LANES : (n + 1) * LANES].reshape(STEPS, SHARD, LANES)

        @pl.when(core == 1)
        def _():
            odd = lax.rem(s, 2)
            keep = lane // 64 == odd
            for f in range(4):
                value = total[:, (f // 2) * LANES : (f // 2 + 1) * LANES]
                value = jnp.where(odd == f % 2, value, turn(value)).reshape(STEPS, SHARD, LANES)
                at = 2 * f + s // 2
                terms[at] = jnp.where(keep.reshape(1, 1, LANES), value, terms[at])

    def panel_product(s):
        panel_half(s, False)
        panel_half(s, True)
        keep_terms(s)

    def term_copy(source, to, g):
        steps = pl.ds(*GROUPS[g])
        return pltpu.make_async_remote_copy(
            src_ref=terms.at[to, steps],
            dst_ref=arrived.at[source, steps],
            send_sem=term_send.at[to, g],
            recv_sem=term_recv.at[source, g],
            device_id={"col": to},
            device_id_type=MESH,
        )

    def give(targets):
        for g in range(len(GROUPS) - 1):
            for to in targets:
                pl.when(to != col)(lambda to=to, g=g: term_copy(col, to, g).start())

    def give_zero(s):
        pl.when(core == 0)(lambda: give([2 * s, 2 * s + 1]))

    def give_one(half):
        pl.when(core == 1)(lambda: give([2 * f + half for f in range(4)]))

    far(FRONT)
    far(BACK)
    panel_product(second)
    give_zero(second)
    for df, parts in ((0, FRONT), (1, FRONT), (3, FRONT), (0, BACK), (1, BACK), (3, BACK), (2, FRONT), (2, BACK)):
        onward(df, parts)

    even = lax.rem(second, 2) == 0
    pair = jnp.where(even, second + 1, second - 1)
    other = wrap(pair + 2)
    panel_product(pair)
    give_zero(pair)
    give_one(second // 2)
    for j in range(2):
        on_own(j, hop)
    panel_product(other)
    give_zero(other)
    for j in range(2, AHEAD):
        on_own(j, hop)
    for df in ORDER:
        last(df, FRONT)
    panel_half(wrap(second + 2), False)
    for j in range(2):
        on_own(j, pass_on)
    for df in ORDER:
        last(df, BACK)
    panel_half(wrap(second + 2), True)
    keep_terms(wrap(second + 2))
    give_zero(wrap(second + 2))
    give_one(1 - second // 2)

    def ready(g):
        begin_at, count = GROUPS[g]
        for d in range(1, COLS):
            term_copy(wrap(col + d, COLS), col, g).wait_recv()
        for k in range(begin_at, begin_at + count):
            value = terms[col, k]
            for d in range(1, COLS):
                value = value + arrived[wrap(col + d, COLS), k]
            own[k] -= value

    def copy(k, d):
        slot = k % 2
        return pltpu.make_async_remote_copy(
            src_ref=own.at[k],
            dst_ref=held.at[slot, row],
            send_sem=send_sem.at[slot, d],
            recv_sem=recv_sem.at[slot, d],
            device_id={"row": wrap(row + d, ROWS)},
            device_id_type=MESH,
        )

    def spread(k):
        for d in PEERS:
            copy(k, d).start()
        held[k % 2, row] = own[k]

    def arrive(k):
        for d in range(1, ROWS):
            copy(k, d).wait_recv()
        high, low = split(held[k % 2].reshape(NB, LANES))
        weights[...] = jnp.concatenate([high, low], axis=1)

    def times(block):
        high, low = split(block)
        both = dot(high, weights[...])
        return both[:, :LANES] + both[:, LANES:] + dot(low, weights[:, :LANES])

    def coupling(k, begin_at, end_at):
        at, _ = pairs_of(k)
        rows = slice(at + begin_at, at + end_at)
        parts = [factor[c, rows, :, :LANES] for c in range(4)] + [factor[c, rows, :, LANES:] for c in (3, 2, 1, 0)]
        return jnp.concatenate([p.reshape(-1, LANES) for p in parts], axis=1)

    ready(0)
    spread(0)
    for k in range(STEPS - 1):
        if k == 0:
            ready(1)
        if k == 2:
            ready(2)
        if k == 5:
            ready(3)
        need(k)
        arrive(k)
        own[k + 1] -= times(coupling(k, 0, 1))
        spread(k + 1)
        if k + 2 < AHEAD:
            on_own(k + 2, pass_on)
        if k == 0:
            for d in range(1, COLS):
                term_copy(col, wrap(col + d, COLS), len(GROUPS) - 1).start()
        if AHEAD <= k + 4 < STEPS - 1:
            on_own(k + 4, share)
        if AHEAD <= k + 2 < STEPS - 1:
            on_own(k + 2, hop)
        if AHEAD <= k + 1 < STEPS - 1:
            on_own(k + 1, pass_on)
        out_ref[k] = times(diag_ref[k])
        for i in range(k + 2, STEPS, 3):
            end_at = min(i + 3, STEPS)
            result = times(coupling(k, i - k - 1, end_at - k - 1))
            own[i:end_at] -= result.reshape(end_at - i, SHARD, LANES)
        for d in range(1, ROWS):
            copy(k, d).wait_send()
    arrive(STEPS - 1)
    out_ref[STEPS - 1] = times(diag_ref[STEPS - 1])

    for d in range(1, ROWS):
        copy(STEPS - 1, d).wait_send()
    for source, part, sent in started:
        guarded(source, part, sent.wait_send)
    for j in range(STEPS - 1):
        on_own(j, lambda j: [factor_copy(j, way, y, partner).wait_send() for way in range(7)] and None)
    for g in range(len(GROUPS)):
        for d in range(1, COLS):
            term_copy(col, wrap(col + d, COLS), g).wait_send()


def on_device(targets, lower_panel, prior_solution, diag_inverse, below_blocks):
    f32, bf16 = jnp.float32, jnp.bfloat16
    vmem = pl.BlockSpec(memory_space=pltpu.VMEM)
    hbm = pl.BlockSpec(memory_space=pl.ANY)
    dma = pltpu.SemaphoreType.DMA
    return pl.pallas_call(
        kernel,
        out_shape=jax.ShapeDtypeStruct(targets.shape, f32),
        in_specs=[vmem, vmem, vmem, hbm, hbm],
        out_specs=vmem,
        scratch_shapes=[
            pltpu.VMEM((ROWS, DIAG + PACKED, LANES), f32),
            pltpu.VMEM((DIAG, PRIOR), bf16),
            pltpu.VMEM((DIAG, PRIOR), bf16),
            pltpu.VMEM((2, STEPS, SHARD, STAGED), f32),
            pltpu.VMEM((4, PAIRS, SHARD, 2 * LANES), f32),
            pltpu.VMEM((DIAG, 2 * LANES), f32),
            pltpu.VMEM((COLS, STEPS, SHARD, LANES), f32),
            pltpu.VMEM((COLS, STEPS, SHARD, LANES), f32),
            pltpu.VMEM((2, ROWS, SHARD, LANES), f32),
            pltpu.VMEM((STEPS, SHARD, LANES), f32),
            pltpu.VMEM((NB, 2 * LANES), bf16),
            pltpu.VMEM((NB, 2 * LANES), bf16),
            pltpu.VMEM((NB, 2 * LANES), bf16),
            dma((15 * len(PARTS),)),
            dma((4, 4, len(PARTS))),
            dma((2, STEPS)),
            dma((STEPS - 1, 7)),
            dma((STEPS - 1, 7)),
            dma((COLS, len(GROUPS))),
            dma((COLS, len(GROUPS))),
            dma((2, ROWS)),
            dma((2, ROWS)),
        ],
        compiler_params=pltpu.CompilerParams(collective_id=0, has_side_effects=True, vmem_limit_bytes=63 << 20),
    )(targets, prior_solution.T, diag_inverse, lower_panel, below_blocks)


def solution(mesh):
    in_specs = (
        P(None, "row", "col"),
        P(None, "row", "col"),
        P("col", "row"),
        P(None, "row", None),
        P(None, "row", None),
    )
    out_specs = P(None, "row", "col")
    return jax.shard_map(
        on_device, mesh=mesh, in_specs=in_specs, out_specs=out_specs, check_vma=False
    )
```

```python
import jax
import jax.numpy as jnp
from jax import lax
from jax.experimental import pallas as pl
from jax.experimental.pallas import tpu as pltpu
from jax.sharding import PartitionSpec as P

MESH = pl.DeviceIdType.MESH
STEPS = 10
ROWS = 16
COLS = 8
NB = 1024
SHARD = 64
LANES = 128
DIAG = STEPS * SHARD
PRIOR = 3712
PACKED = PRIOR // 2
SLAB = 512
SLABS = PRIOR // SLAB
TAIL = PRIOR - SLABS * SLAB
TAKEN = (STEPS // 2) * SHARD
EARLY = 1024
LATE = PACKED - EARLY
PARTS = (
    (0, 128),
    (128, 128),
    (256, 64),
    (TAKEN, 128),
    (TAKEN + 128, 128),
    (TAKEN + 256, 64),
    (DIAG, EARLY // 2),
    (DIAG + EARLY // 2, EARLY // 2),
    (DIAG + EARLY, LATE // 2),
    (DIAG + EARLY + LATE // 2, LATE // 2),
)
SMALL, FRONT, BACK = (0, 1, 2, 3, 4, 5), (6, 7), (8, 9)
ORDER = (0, 1, 3, 2)
PEERS = (10, 6, 14, 9, 11, 5, 15, 7, 13, 8, 2, 4, 1, 12, 3)
PAIRS = STEPS * (STEPS - 1) // 2
STAGED = 1024
GROUPS = ((0, 1), (1, 2), (3, 3), (6, 4))
AHEAD = 4


def split(value):
    high = value.astype(jnp.bfloat16)
    return high, (value - high.astype(jnp.float32)).astype(jnp.bfloat16)


def dot(left, right):
    return jnp.dot(left, right, preferred_element_type=jnp.float32)


def pairs_of(j):
    return (STEPS - 1) * j - j * (j - 1) // 2, STEPS - 1 - j


def wrap(value, size=4):
    return lax.rem(value + size, size)


def kernel(
    target_ref, prior_ref, diag_ref, panel_ref, below_ref, out_ref,
    blocks, panel_high, panel_low, stage, factor, total, terms, arrived, held, own, weights, wide_high, wide_low,
    block_send, block_recv, stage_sem, factor_send, factor_recv, term_send, term_recv, send_sem, recv_sem,
):
    row = lax.axis_index("row")
    col = lax.axis_index("col")
    z, x = row // 4, lax.rem(row, 4)
    y, core = col // 2, lax.rem(col, 2)
    swap = core == 1
    second = jnp.where(swap, x, z)
    groups = (y, 7 - y)
    lane = lax.broadcasted_iota(jnp.int32, (1, LANES), 1)
    low_lanes = lane < 64

    def turn(value):
        return pltpu.roll(value, 64, 1)

    def panel_copy(q):
        width = min(STAGED, PRIOR - q * STAGED)
        return pltpu.make_async_copy(
            panel_ref.at[:, :, pl.ds(q * STAGED, width)], stage.at[q % 2, :, :, pl.ds(0, width)], stage_sem.at[q % 2, 0]
        )

    def below_copy(j, i):
        slot = j // 2 % 2
        return pltpu.make_async_copy(below_ref.at[i * (i - 1) // 2 + j], stage.at[slot, i], stage_sem.at[slot, i])

    panel_copy(0).start()
    panel_copy(1).start()

    barrier = pltpu.get_barrier_semaphore()
    for d in range(1, ROWS):
        pl.semaphore_signal(barrier, inc=1, device_id={"row": wrap(row + d, ROWS)}, device_id_type=MESH)
    for d in range(1, COLS):
        pl.semaphore_signal(barrier, inc=1, device_id={"col": wrap(col + d, COLS)}, device_id_type=MESH)

    for n in range(2):
        lanes = pl.ds(pl.multiple_of(groups[n] * LANES, LANES), LANES)
        for t in range(STEPS // 2):
            blocks[row, n * TAKEN + t * SHARD : n * TAKEN + (t + 1) * SHARD] = diag_ref[2 * t + core, :, lanes]
    for m in range(SLABS):
        piece = jnp.concatenate(
            [prior_ref[:, m * SLAB : m * SLAB + 256], prior_ref[:, m * SLAB + 256 : (m + 1) * SLAB]], axis=0
        )
        blocks[row, DIAG + 256 * m : DIAG + 256 * (m + 1)] = piece.T
    piece = prior_ref[:, SLABS * SLAB :].T
    blocks[row, DIAG + 256 * SLABS :] = jnp.concatenate([piece[:64], piece[64:]], axis=1)
    own[...] = target_ref[...]

    pl.semaphore_wait(barrier, ROWS + COLS - 2)

    def turned_of(part):
        return jnp.bool_(True) if part in (3, 4, 5) else swap

    def place(part):
        turned = turned_of(part)
        return jnp.where(turned, x, z), jnp.where(turned, z, x)

    def row_of(part, s, f):
        s, f = wrap(s), wrap(f)
        return jnp.where(turned_of(part), f * 4 + s, s * 4 + f)

    started = []

    def guarded(source, part, action):
        if part in SMALL:
            needed = source >= 2 * groups[part // 3]
            pl.when(jnp.logical_and(needed, core == 0) if part in (2, 5) else needed)(action)
        else:
            action()

    def send(part, to_s, to_f, ds, df):
        s, f = place(part)
        source = row_of(part, s + to_s - ds, f + to_f - df)
        piece = blocks.at[source, pl.ds(*PARTS[part])]
        copy = pltpu.make_async_remote_copy(
            src_ref=piece,
            dst_ref=piece,
            send_sem=block_send.at[len(started)],
            recv_sem=block_recv.at[ds, df, part],
            device_id={"row": row_of(part, s + to_s, f + to_f)},
            device_id_type=MESH,
        )
        guarded(source, part, copy.start)
        started.append((source, part, copy))

    def wait(part, ds, df):
        s, f = place(part)
        source = row_of(part, s - ds, f - df)
        piece = blocks.at[source, pl.ds(*PARTS[part])]
        copy = pltpu.make_async_remote_copy(
            src_ref=piece,
            dst_ref=piece,
            send_sem=block_send.at[0],
            recv_sem=block_recv.at[ds, df, part],
            device_id={"row": row_of(part, s + 1, f)},
            device_id_type=MESH,
        )
        guarded(source, part, copy.wait_recv)

    def up(df, part):
        send(part, 1, 0, 1, df)
        send(part, -1, 0, 3, df)

    def begin(parts):
        for part in parts:
            send(part, 0, 1, 0, 1)
            send(part, 0, -1, 0, 3)
            up(0, part)

    def near(parts):
        for part in parts:
            wait(part, 0, 1)
            if part % 2 == 0:
                send(part, 0, 1, 0, 2)
            up(1, part)
            wait(part, 0, 3)
            if part % 2 == 1:
                send(part, 0, -1, 0, 2)
            up(3, part)

    def far(parts):
        for part in parts:
            wait(part, 0, 2)
            up(2, part)

    def onward(df, parts):
        for part in parts:
            wait(part, 1, df)
            wait(part, 3, df)
            if part % 2 == 0:
                send(part, 1, 0, 2, df)
            else:
                send(part, -1, 0, 2, df)

    def last(df, parts):
        for part in parts:
            wait(part, 2, df)

    begin(SMALL)

    def convert(q):
        panel_copy(q).wait()
        width = min(STAGED, PRIOR - q * STAGED)
        for k in range(STEPS):
            high, low = split(stage[q % 2, k, :, :width])
            panel_high[k * SHARD : (k + 1) * SHARD, q * STAGED : q * STAGED + width] = high
            panel_low[k * SHARD : (k + 1) * SHARD, q * STAGED : q * STAGED + width] = low
        if q + 2 < 4:
            panel_copy(q + 2).start()

    convert(0)
    convert(1)
    near(SMALL)
    far(SMALL)
    begin(FRONT)
    begin(BACK)
    convert(2)
    convert(3)

    def below_start(j):
        for i in range(j + 1, STEPS):
            below_copy(j, i).start()

    def on_own(j, action):
        if j < STEPS - 1:
            pl.when(core == j % 2)(lambda: action(j))

    for j in range(4):
        on_own(j, below_start)

    for df in ORDER:
        onward(df, SMALL)
    near(FRONT)
    for df in ORDER:
        last(df, SMALL)

    def factor_copy(j, way, source, to):
        at, count = pairs_of(j)
        part = factor.at[source, pl.ds(at, count)]
        return pltpu.make_async_remote_copy(
            src_ref=part,
            dst_ref=part,
            send_sem=factor_send.at[j, way],
            recv_sem=factor_recv.at[j, way],
            device_id={"col": to},
            device_id_type=MESH,
        )

    def at_y(dy):
        return wrap(y + dy)

    same = lambda dy: at_y(dy) * 2 + core
    partner = y * 2 + 1 - core

    def share(j):
        factor_copy(j, 1, y, same(1)).start()
        factor_copy(j, 2, y, same(-1)).start()
        factor_copy(j, 0, y, partner).start()

    def make_factor(j):
        t = j // 2
        for n in range(2):
            for r in range(ROWS):
                value = blocks[r, n * TAKEN + t * SHARD : n * TAKEN + (t + 1) * SHARD]
                high, low = split(jnp.where(r >= 2 * groups[n], value, 0.0))
                wide_high[r * SHARD : (r + 1) * SHARD, n * LANES : (n + 1) * LANES] = high
                wide_low[r * SHARD : (r + 1) * SHARD, n * LANES : (n + 1) * LANES] = low
        at, count = pairs_of(j)
        for i in range(j + 1, STEPS):
            below_copy(j, i).wait()
        for begin_at in range(0, count, 3):
            n = min(3, count - begin_at)
            i = j + 1 + begin_at
            high, low = split(stage[t % 2, i : i + n].reshape(n * SHARD, NB))
            result = dot(high, wide_high[...]) + dot(high, wide_low[...]) + dot(low, wide_high[...])
            factor[y, at + begin_at : at + begin_at + n] = result.reshape(n, SHARD, 2 * LANES)
        if j + 4 < STEPS - 1:
            below_start(j + 4)
        if j < AHEAD:
            share(j)

    for j in range(STEPS - 1):
        on_own(j, make_factor)
    near(BACK)

    def up_goes(j):
        return j // 2 % 2 == 0

    def hop(j):
        way, dy = (1, -1) if up_goes(j) else (2, 1)
        factor_copy(j, way, at_y(dy), same(-dy)).wait_recv()
        factor_copy(j, 3, at_y(dy), same(-dy)).start()
        factor_copy(j, 3 + way, at_y(dy), partner).start()

    def pass_on(j):
        way, dy = (2, 1) if up_goes(j) else (1, -1)
        factor_copy(j, way, at_y(dy), same(1)).wait_recv()
        factor_copy(j, 3 + way, at_y(dy), partner).start()
        factor_copy(j, 3, at_y(2), same(1)).wait_recv()
        factor_copy(j, 6, at_y(2), partner).start()

    def need(j):
        @pl.when(core != j % 2)
        def _():
            for way, dy in ((0, 0), (4, -1), (5, 1), (6, 2)):
                factor_copy(j, way, at_y(dy), partner).wait_recv()

    def slab_weights(rows_of, height):
        parts = [rows_of(f) for f in range(4)]
        turned = [turn(p) for p in parts]
        upper = [jnp.where(low_lanes, parts[f], turned[f + 1]) for f in (0, 2)]
        lower = [jnp.where(low_lanes, turned[f], parts[f + 1]) for f in (0, 2)]
        for side_at, values in ((0, upper), (height, lower)):
            for n in range(2):
                high, low = split(values[n])
                wide_high[side_at : side_at + height, n * LANES : (n + 1) * LANES] = high
                wide_low[side_at : side_at + height, n * LANES : (n + 1) * LANES] = low

    def panel_term(columns, depth):
        high = panel_high[:, columns]
        return (
            dot(high, wide_high[:depth])
            + dot(high, wide_low[:depth])
            + dot(panel_low[:, columns], wide_high[:depth])
        )

    def group_row(s, f):
        return jnp.where(swap, f * 4 + s, s * 4 + f)

    def panel_half(s, back):
        def slab(m, carry):
            at = pl.multiple_of(DIAG + 256 * m, LANES)
            slab_weights(lambda f: blocks[group_row(s, f), pl.ds(at, 256)], 256)
            total[...] += panel_term(pl.ds(pl.multiple_of(m * SLAB, SLAB), SLAB), SLAB)
            return carry

        if back:
            slab_weights(lambda f: blocks[group_row(s, f), DIAG + 256 * SLABS :], 64)
            total[...] += panel_term(pl.ds(SLABS * SLAB, TAIL), TAIL)
            lax.fori_loop(EARLY // 256, SLABS, slab, 0)
        else:
            total[...] = jnp.zeros_like(total)
            lax.fori_loop(0, EARLY // 256, slab, 0)

    def keep_terms(s):
        @pl.when(core == 0)
        def _():
            for n in range(2):
                terms[2 * s + n] = total[:, n * LANES : (n + 1) * LANES].reshape(STEPS, SHARD, LANES)

        @pl.when(core == 1)
        def _():
            odd = lax.rem(s, 2)
            keep = lane // 64 == odd
            for f in range(4):
                value = total[:, (f // 2) * LANES : (f // 2 + 1) * LANES]
                value = jnp.where(odd == f % 2, value, turn(value)).reshape(STEPS, SHARD, LANES)
                at = 2 * f + s // 2
                terms[at] = jnp.where(keep.reshape(1, 1, LANES), value, terms[at])

    def panel_product(s):
        panel_half(s, False)
        panel_half(s, True)
        keep_terms(s)

    def term_copy(source, to, g):
        steps = pl.ds(*GROUPS[g])
        return pltpu.make_async_remote_copy(
            src_ref=terms.at[to, steps],
            dst_ref=arrived.at[source, steps],
            send_sem=term_send.at[to, g],
            recv_sem=term_recv.at[source, g],
            device_id={"col": to},
            device_id_type=MESH,
        )

    def give(targets):
        for g in range(len(GROUPS) - 1):
            for to in targets:
                pl.when(to != col)(lambda to=to, g=g: term_copy(col, to, g).start())

    def give_zero(s):
        pl.when(core == 0)(lambda: give([2 * s, 2 * s + 1]))

    def give_one(half):
        pl.when(core == 1)(lambda: give([2 * f + half for f in range(4)]))

    far(FRONT)
    far(BACK)
    panel_product(second)
    give_zero(second)
    for df, parts in ((0, FRONT), (1, FRONT), (3, FRONT), (0, BACK), (1, BACK), (3, BACK), (2, FRONT), (2, BACK)):
        onward(df, parts)

    even = lax.rem(second, 2) == 0
    pair = jnp.where(even, second + 1, second - 1)
    other = wrap(pair + 2)
    for j in range(2):
        on_own(j, hop)
    panel_product(pair)
    give_zero(pair)
    give_one(second // 2)
    for j in range(2, AHEAD):
        on_own(j, hop)
    panel_product(other)
    give_zero(other)
    for j in range(2):
        on_own(j, pass_on)
    for df in ORDER:
        last(df, FRONT)
    panel_half(wrap(second + 2), False)
    for j in range(2, AHEAD):
        on_own(j, pass_on)
    for df in ORDER:
        last(df, BACK)
    panel_half(wrap(second + 2), True)
    keep_terms(wrap(second + 2))
    give_zero(wrap(second + 2))
    give_one(1 - second // 2)

    def ready(g):
        begin_at, count = GROUPS[g]
        for d in range(1, COLS):
            term_copy(wrap(col + d, COLS), col, g).wait_recv()
        for k in range(begin_at, begin_at + count):
            value = terms[col, k]
            for d in range(1, COLS):
                value = value + arrived[wrap(col + d, COLS), k]
            own[k] -= value

    def copy(k, d):
        slot = k % 2
        return pltpu.make_async_remote_copy(
            src_ref=own.at[k],
            dst_ref=held.at[slot, row],
            send_sem=send_sem.at[slot, d],
            recv_sem=recv_sem.at[slot, d],
            device_id={"row": wrap(row + d, ROWS)},
            device_id_type=MESH,
        )

    def spread(k):
        for d in PEERS:
            copy(k, d).start()
        held[k % 2, row] = own[k]

    def arrive(k):
        for d in range(1, ROWS):
            copy(k, d).wait_recv()
        high, low = split(held[k % 2].reshape(NB, LANES))
        weights[...] = jnp.concatenate([high, low], axis=1)

    def times(block):
        high, low = split(block)
        both = dot(high, weights[...])
        return both[:, :LANES] + both[:, LANES:] + dot(low, weights[:, :LANES])

    def coupling(k, begin_at, end_at):
        at, _ = pairs_of(k)
        rows = slice(at + begin_at, at + end_at)
        parts = [factor[c, rows, :, :LANES] for c in range(4)] + [factor[c, rows, :, LANES:] for c in (3, 2, 1, 0)]
        return jnp.concatenate([p.reshape(-1, LANES) for p in parts], axis=1)

    ready(0)
    spread(0)
    for k in range(STEPS - 1):
        if k == 0:
            ready(1)
        if k == 2:
            ready(2)
        if k == 5:
            ready(3)
        need(k)
        arrive(k)
        own[k + 1] -= times(coupling(k, 0, 1))
        spread(k + 1)
        if k == 0:
            for d in range(1, COLS):
                term_copy(col, wrap(col + d, COLS), len(GROUPS) - 1).start()
        if AHEAD <= k + 4 < STEPS - 1:
            on_own(k + 4, share)
        if AHEAD <= k + 2 < STEPS - 1:
            on_own(k + 2, hop)
        if AHEAD <= k + 1 < STEPS - 1:
            on_own(k + 1, pass_on)
        out_ref[k] = times(diag_ref[k])
        for i in range(k + 2, STEPS, 3):
            end_at = min(i + 3, STEPS)
            result = times(coupling(k, i - k - 1, end_at - k - 1))
            own[i:end_at] -= result.reshape(end_at - i, SHARD, LANES)
        for d in range(1, ROWS):
            copy(k, d).wait_send()
    arrive(STEPS - 1)
    out_ref[STEPS - 1] = times(diag_ref[STEPS - 1])

    for d in range(1, ROWS):
        copy(STEPS - 1, d).wait_send()
    for source, part, sent in started:
        guarded(source, part, sent.wait_send)
    for j in range(STEPS - 1):
        on_own(j, lambda j: [factor_copy(j, way, y, partner).wait_send() for way in range(7)] and None)
    for g in range(len(GROUPS)):
        for d in range(1, COLS):
            term_copy(col, wrap(col + d, COLS), g).wait_send()


def on_device(targets, lower_panel, prior_solution, diag_inverse, below_blocks):
    f32, bf16 = jnp.float32, jnp.bfloat16
    vmem = pl.BlockSpec(memory_space=pltpu.VMEM)
    hbm = pl.BlockSpec(memory_space=pl.ANY)
    dma = pltpu.SemaphoreType.DMA
    return pl.pallas_call(
        kernel,
        out_shape=jax.ShapeDtypeStruct(targets.shape, f32),
        in_specs=[vmem, vmem, vmem, hbm, hbm],
        out_specs=vmem,
        scratch_shapes=[
            pltpu.VMEM((ROWS, DIAG + PACKED, LANES), f32),
            pltpu.VMEM((DIAG, PRIOR), bf16),
            pltpu.VMEM((DIAG, PRIOR), bf16),
            pltpu.VMEM((2, STEPS, SHARD, STAGED), f32),
            pltpu.VMEM((4, PAIRS, SHARD, 2 * LANES), f32),
            pltpu.VMEM((DIAG, 2 * LANES), f32),
            pltpu.VMEM((COLS, STEPS, SHARD, LANES), f32),
            pltpu.VMEM((COLS, STEPS, SHARD, LANES), f32),
            pltpu.VMEM((2, ROWS, SHARD, LANES), f32),
            pltpu.VMEM((STEPS, SHARD, LANES), f32),
            pltpu.VMEM((NB, 2 * LANES), bf16),
            pltpu.VMEM((NB, 2 * LANES), bf16),
            pltpu.VMEM((NB, 2 * LANES), bf16),
            dma((15 * len(PARTS),)),
            dma((4, 4, len(PARTS))),
            dma((2, STEPS)),
            dma((STEPS - 1, 7)),
            dma((STEPS - 1, 7)),
            dma((COLS, len(GROUPS))),
            dma((COLS, len(GROUPS))),
            dma((2, ROWS)),
            dma((2, ROWS)),
        ],
        compiler_params=pltpu.CompilerParams(collective_id=0, has_side_effects=True, vmem_limit_bytes=63 << 20),
    )(targets, prior_solution.T, diag_inverse, lower_panel, below_blocks)


def solution(mesh):
    in_specs = (
        P(None, "row", "col"),
        P(None, "row", "col"),
        P("col", "row"),
        P(None, "row", None),
        P(None, "row", None),
    )
    out_specs = P(None, "row", "col")
    return jax.shard_map(
        on_device, mesh=mesh, in_specs=in_specs, out_specs=out_specs, check_vma=False
    )
```
